256 devices in a mesh: ctx: 32 (over y_hi, z, core), head: 8 (over y_lo, x).
Axes of the slice: x: 4, y: 4 (y_hi: 2, y_lo: 2; y = y_hi * 2 + y_lo), z: 8, core: 2. Of those that a mesh axis runs over, the one named last changes fastest.
Arguments:
- queries: bfloat16 [16384, 4096], P(('ctx', 'head')), may hold values from -5.5 to 5.5
- keys: bfloat16 [16384, 1024], P(('ctx', 'head')), may hold values from -5.5 to 5.5
- values: bfloat16 [16384, 1024], P(('ctx', 'head')), may hold values from -6 to 6
- block_order: int32 [64], replicated, may hold values from 0 to 63, each once
Outputs:
- attended: bfloat16 [16384, 4096], P(('ctx', 'head'))
The draws below stay inside these ranges and needn't reach their ends.
Inputs may be any that keep to these rules, and one draw needn't show every extreme that they name: `block_order`: each number appears once.
All inputs are finite; a program needn't handle non-finite values.
Results may differ from the reference program's by a relative error of at most 0.007.
Values may be sent and summed in bfloat16 or wider, within the bound.
No kernel may reach another device: no remote copies, remote signals or barrier semaphores. Data moves between devices by JAX's collectives and lax.ppermute only.
A program may use at most 64 MiB of HBM per device.

```python
import jax
import jax.numpy as jnp
from jax import lax

Q_HEADS = 32
KV_HEADS = 8
HEAD_DIM = 128
BLOCK = 256
BLOCKS = 64
LENGTH = 16384


def draw_queries(key, part):
    key = jax.random.fold_in(key, 1)
    drawn = jnp.clip(jax.random.normal(key, (LENGTH, Q_HEADS * HEAD_DIM), jnp.float32), -4.0, 4.0)
    return drawn.astype(jnp.bfloat16)


def draw_keys(key, part):
    key = jax.random.fold_in(key, 2)
    drawn = jnp.clip(jax.random.normal(key, (LENGTH, KV_HEADS * HEAD_DIM), jnp.float32), -4.0, 4.0)
    return drawn.astype(jnp.bfloat16)


def block_levels(stream_key, shape, pieces, least, top_value):
    gain, own = 1.0, jax.random.fold_in(stream_key, 6)
    for dim, parts in pieces:
        heights = jnp.exp(jax.random.uniform(jax.random.fold_in(own, dim), (parts,), jnp.float32, least / len(pieces), top_value / len(pieces)))
        gain = gain * jnp.repeat(heights, shape[dim] // parts).reshape([-1 if axis == dim else 1 for axis in range(len(shape))])
    return gain


def scatter_about(key, extent, deviation, bound, cuts=(), kind=jnp.bfloat16):
    values = deviation * jax.random.normal(key, extent, jnp.float32)
    if cuts:
        values = values * block_levels(key, extent, cuts, -0.22, 0.18)
    return jnp.clip(values, -bound, bound).astype(kind)


def setup_inputs(seed: int = 0) -> dict:
    key_of = jax.random.split(jax.random.key(seed), 5)
    return {
        "queries": draw_queries(jax.random.fold_in(key_of[4], 71), 0),
        "keys": draw_keys(jax.random.fold_in(key_of[4], 71), 0),
        "values": scatter_about(key_of[2], (LENGTH, KV_HEADS * HEAD_DIM), 1.0, 6.0, ((0, 256),)),
        "block_order": jax.random.permutation(key_of[3], BLOCKS).astype(jnp.int32),
    }


def reference(queries, keys, values, block_order):
    row_ids = jnp.arange(LENGTH, dtype=jnp.int32)
    positions = block_order[row_ids // BLOCK] * BLOCK + row_ids % BLOCK
    visible = positions[None, :] <= positions[:, None]
    groups = Q_HEADS // KV_HEADS
    query_heads = queries.reshape(LENGTH, Q_HEADS, HEAD_DIM).transpose(1, 0, 2)
    key_heads = keys.reshape(LENGTH, KV_HEADS, HEAD_DIM).transpose(1, 0, 2)
    value_heads = values.reshape(LENGTH, KV_HEADS, HEAD_DIM).transpose(1, 0, 2)

    def per_head(head_index):
        query_one = query_heads[head_index]
        key_one = key_heads[head_index // groups]
        value_one = value_heads[head_index // groups]
        scores = jnp.dot(query_one, key_one.T, preferred_element_type=jnp.float32) * (HEAD_DIM ** -0.5)
        row_max = jnp.max(jnp.where(visible, scores, -1e30), axis=1, keepdims=True)
        expos = jnp.where(visible, jnp.exp(scores - row_max), 0.0)
        totals = jnp.sum(expos, axis=1, keepdims=True)
        summed = jnp.dot(expos.astype(jnp.bfloat16), value_one, preferred_element_type=jnp.float32)
        return summed / totals

    result = lax.map(per_head, jnp.arange(Q_HEADS, dtype=jnp.int32))
    return result.transpose(1, 0, 2).reshape(LENGTH, Q_HEADS * HEAD_DIM).astype(jnp.bfloat16)
```

```python
import functools

import jax
import jax.numpy as jnp
import numpy as np
from jax import lax
from jax.experimental import pallas as pl
from jax.experimental.pallas import tpu as pltpu
from jax.sharding import Mesh
from jax.sharding import PartitionSpec as P

HEAD_DIM = 128
BLOCK = 256
ROWS = 2 * BLOCK
BLOCKS = 4
EXTENDED = HEAD_DIM + 16
NEG = -1e30
LOG2E_SCALE = float(np.log2(np.e) / np.sqrt(HEAD_DIM))
AXES = ("yh", "z", "c", "yl", "x")
F32 = jnp.float32
BF16 = jnp.bfloat16
SMEM = pl.BlockSpec(memory_space=pltpu.SMEM)
VMEM = pl.BlockSpec(memory_space=pltpu.VMEM)
ANY = pl.BlockSpec(memory_space=pl.ANY)
VMEM_BYTES = 48 * 2**20


def nt(a, b):
    return lax.dot_general(a, b, (((1,), (0,)), ((), ())), preferred_element_type=F32)


def prepare_kernel(got_ref, q_ref, kv_ref):
    for b in range(BLOCKS):
        for h in range(2):
            q_ref[b, :, h * BLOCK : (h + 1) * BLOCK] = got_ref[
                b, :, h * HEAD_DIM : (h + 1) * HEAD_DIM
            ].T
        kv_ref[b, :BLOCK] = got_ref[b, :, 2 * HEAD_DIM : 3 * HEAD_DIM]
        value = got_ref[b, :, 3 * HEAD_DIM :].T
        kv_ref[b, BLOCK : BLOCK + HEAD_DIM] = value[:, :HEAD_DIM]
        kv_ref[b, BLOCK + HEAD_DIM :] = value[:, HEAD_DIM:]


def prepare(got):
    return pl.pallas_call(
        prepare_kernel,
        out_shape=(
            jax.ShapeDtypeStruct((BLOCKS, HEAD_DIM, ROWS), BF16),
            jax.ShapeDtypeStruct((BLOCKS, 2 * BLOCK, HEAD_DIM), BF16),
        ),
        in_specs=[VMEM],
        out_specs=(VMEM, VMEM),
        name="prepare",
    )(got)


def value_of(kv_ref, t):
    return jnp.concatenate(
        [kv_ref[t, BLOCK : BLOCK + HEAD_DIM], kv_ref[t, BLOCK + HEAD_DIM :]], axis=1
    )


def own_kernel(meta_ref, order_ref, q_ref, kv_ref, m_ref, acc_ref):
    first = (meta_ref[0] * 8 + meta_ref[1]) * BLOCKS
    values = jnp.concatenate([value_of(kv_ref, t) for t in range(BLOCKS)], axis=1)
    lhs = jnp.concatenate([values, jnp.ones((16, BLOCKS * BLOCK), BF16)], axis=0)
    keys = jnp.concatenate([kv_ref[t, :BLOCK] for t in range(BLOCKS)], axis=0)
    row = lax.broadcasted_iota(jnp.int32, (BLOCK, ROWS), 0)
    col = lax.broadcasted_iota(jnp.int32, (BLOCK, ROWS), 1) & (BLOCK - 1)
    ahead = row - col
    for i in range(BLOCKS):
        scores = nt(keys, q_ref[i]) * LOG2E_SCALE
        q_pos = order_ref[first + i] * BLOCK
        parts = []
        for t in range(BLOCKS):
            part = scores[t * BLOCK : (t + 1) * BLOCK]
            room = q_pos - order_ref[first + t] * BLOCK
            parts.append(jnp.where(ahead <= room, part, NEG))
        scores = jnp.concatenate(parts, axis=0)
        row_max = jnp.max(scores, axis=0, keepdims=True)
        m_ref[i] = row_max
        acc_ref[i] = nt(lhs, jnp.exp2(scores - row_max).astype(BF16))


def own_start(meta, order, q, kv):
    return pl.pallas_call(
        own_kernel,
        out_shape=(
            jax.ShapeDtypeStruct((BLOCKS, 1, ROWS), F32),
            jax.ShapeDtypeStruct((BLOCKS, EXTENDED, ROWS), F32),
        ),
        in_specs=[SMEM, SMEM, VMEM, VMEM],
        out_specs=(VMEM, VMEM),
        compiler_params=pltpu.CompilerParams(vmem_limit_bytes=VMEM_BYTES),
        cost_estimate=pl.CostEstimate(
            flops=16 * 4 * BLOCK * ROWS * 256, bytes_accessed=4 << 20, transcendentals=2 << 20
        ),
        name="own_start",
    )(meta, order, q, kv)


def attend_kernel(steps, starts, final, *refs):
    count = len(steps)
    meta_ref, order_ref, q_ref = refs[:3]
    kv_refs = refs[3 : 3 + count]
    rest = refs[3 + count :]
    if not starts:
        m_in, acc_in = rest[:2]
        rest = rest[2:]
    if final:
        out_ref, m_ref, acc_ref = rest[:3]
        rest = rest[3:]
    else:
        m_ref, acc_ref = rest[:2]
        rest = rest[2:]
    kv_s, scores_a, scores_b, max_a, max_b, item_q, item_k, item_v, item_f, sems = rest

    copies = []
    at = 0
    for n, (size, _, _) in enumerate(steps):
        copies.append(pltpu.make_async_copy(kv_refs[n], kv_s.at[pl.ds(at, size)], sems.at[n]))
        copies[-1].start()
        at += size
    total = at
    kv_s[total] = jnp.zeros((2 * BLOCK, HEAD_DIM), BF16)
    if starts:
        m_ref[...] = jnp.full(m_ref.shape, NEG, F32)
        acc_ref[...] = jnp.zeros(acc_ref.shape, F32)
    else:
        m_ref[...] = m_in[...]
        acc_ref[...] = acc_in[...]

    yh, z, c = meta_ref[0], meta_ref[1], meta_ref[2]
    up = 2 * c - 1
    q_side = 1 - yh if starts or final else yh
    q_first = (q_side * 8 + z) * BLOCKS

    begin = 0
    for i in range(BLOCKS):
        q_pos = order_ref[q_first + i]
        fill = begin
        t = 0
        for size, distance, half in steps:
            plane = (z + up * distance + 16) & 7
            base = (yh * 8 + plane) * BLOCKS
            if size < BLOCKS:
                base = base + (c if half == 0 else 1 - c) * size
            for b in range(size):
                item_q[fill >> 1] = i
                item_k[fill] = t
                item_v[fill] = t
                item_f[fill] = 1.0
                fill = fill + jnp.where(order_ref[base + b] < q_pos, 1, 0)
                t += 1
        last = item_k[jnp.maximum(fill - 1, 0)]
        item_k[fill] = last
        item_v[fill] = total
        item_f[fill] = 0.0
        begin = begin + (((fill - begin) + 1) >> 1) * 2
    items = begin >> 1
    back = jnp.maximum(items - 1, 0)
    again_q, again_k, again_l = item_q[back], item_k[2 * back], item_k[2 * back + 1]
    again_q = jnp.where(items > 0, again_q, 0)
    again_k = jnp.where(items > 0, again_k, 0)
    again_l = jnp.where(items > 0, again_l, 0)
    for n in range(2):
        item_q[items + n] = again_q
        item_k[2 * (items + n)] = again_k
        item_k[2 * (items + n) + 1] = again_l
        item_v[2 * (items + n)] = total
        item_v[2 * (items + n) + 1] = total
        item_f[2 * (items + n)] = 0.0
        item_f[2 * (items + n) + 1] = 0.0

    for copy in copies:
        copy.wait()

    halves = [slice(0, BLOCK), slice(BLOCK, ROWS)]

    def score(j, scores, maxima, cols):
        keys = jnp.concatenate([kv_s[item_k[2 * j], :BLOCK], kv_s[item_k[2 * j + 1], :BLOCK]], 0)
        s = nt(keys, q_ref[item_q[j], :, cols]) * LOG2E_SCALE
        scores[:, cols] = s
        maxima[:, cols] = jnp.max(s, axis=0, keepdims=True)

    def absorb(j, scores, maxima, cols):
        i = item_q[j]
        values = jnp.concatenate([value_of(kv_s, item_v[2 * j + n]) for n in range(2)], axis=1)
        ones = jnp.concatenate(
            [jnp.full((16, BLOCK), item_f[2 * j + n], F32).astype(BF16) for n in range(2)], axis=1
        )
        lhs = jnp.concatenate([values, ones], axis=0)
        old = m_ref[i, :, cols]
        new = jnp.maximum(old, maxima[:, cols])
        keep = jnp.exp2(old - new)
        m_ref[i, :, cols] = new
        p = jnp.exp2(scores[:, cols] - new).astype(BF16)
        acc_ref[i, :, cols] = acc_ref[i, :, cols] * keep + nt(lhs, p)

    def both(j, scores, maxima, next_scores, next_maxima):
        for cols in halves:
            score(j + 1, next_scores, next_maxima, cols)
            absorb(j, scores, maxima, cols)

    for cols in halves:
        score(0, scores_a, max_a, cols)

    def two_items(h, carry):
        both(2 * h, scores_a, max_a, scores_b, max_b)
        both(2 * h + 1, scores_b, max_b, scores_a, max_a)
        return carry

    lax.fori_loop(0, (items + 1) >> 1, two_items, 0)

    if final:
        sub = lax.broadcasted_iota(jnp.int32, (16, ROWS), 0)
        for i in range(BLOCKS):
            sums = acc_ref[i, HEAD_DIM : HEAD_DIM + 1]
            some = sums > 0.0
            safe = jnp.where(some, sums, 1.0)
            logs = jnp.where(some, m_ref[i] + jnp.log2(safe), NEG)
            high = logs.astype(BF16).astype(F32)
            middle = (logs - high).astype(BF16).astype(F32)
            low = logs - high - middle
            out_ref[i, :HEAD_DIM] = (acc_ref[i, :HEAD_DIM] * (1.0 / safe)).astype(BF16)
            out_ref[i, HEAD_DIM:] = jnp.where(
                sub == 0, high, jnp.where(sub == 1, middle, jnp.where(sub == 2, low, 0.0))
            ).astype(BF16)


def attend(meta, order, q, shards, state, final):
    steps = tuple((a.shape[0], distance, half) for a, distance, half in shards)
    total = sum(s[0] for s in steps)
    starts = state is None
    args = [meta, order, q] + [a for a, _, _ in shards] + ([] if starts else list(state))
    m_shape, acc_shape = (BLOCKS, 1, ROWS), (BLOCKS, EXTENDED, ROWS)
    work = [pltpu.VMEM(m_shape, F32), pltpu.VMEM(acc_shape, F32)]
    if final:
        out_shape = (jax.ShapeDtypeStruct(acc_shape, BF16),)
    else:
        out_shape = (jax.ShapeDtypeStruct(m_shape, F32), jax.ShapeDtypeStruct(acc_shape, F32))
        work = []
    pairs = BLOCKS * total // 2
    slots = 2 * (BLOCKS * ((total + 1) // 2) + 4)
    got = pl.pallas_call(
        functools.partial(attend_kernel, steps, starts, final),
        out_shape=out_shape,
        in_specs=[SMEM, SMEM, VMEM] + [ANY] * len(shards) + ([] if starts else [VMEM, VMEM]),
        out_specs=tuple(VMEM for _ in out_shape),
        scratch_shapes=work
        + [
            pltpu.VMEM((total + 1, 2 * BLOCK, HEAD_DIM), BF16),
            pltpu.VMEM((2 * BLOCK, ROWS), F32),
            pltpu.VMEM((2 * BLOCK, ROWS), F32),
            pltpu.VMEM((1, ROWS), F32),
            pltpu.VMEM((1, ROWS), F32),
            pltpu.SMEM((slots // 2,), jnp.int32),
            pltpu.SMEM((slots,), jnp.int32),
            pltpu.SMEM((slots,), jnp.int32),
            pltpu.SMEM((slots,), F32),
            pltpu.SemaphoreType.DMA((len(shards),)),
        ],
        compiler_params=pltpu.CompilerParams(vmem_limit_bytes=VMEM_BYTES),
        cost_estimate=pl.CostEstimate(
            flops=pairs * 4 * BLOCK * ROWS * 256,
            bytes_accessed=6 << 20,
            transcendentals=pairs * BLOCK * ROWS,
        ),
        name="attend",
    )(*args)
    return got[0] if final else got


def combine_kernel(m_ref, acc_ref, other_ref, out_ref):
    for i in range(BLOCKS):
        sums = acc_ref[i, HEAD_DIM : HEAD_DIM + 1]
        mine = m_ref[i] + jnp.log2(sums)
        tail = other_ref[i, HEAD_DIM:].astype(F32)
        theirs = tail[0:1] + tail[1:2] + tail[2:3]
        top = jnp.maximum(mine, theirs)
        weight_mine, weight_theirs = jnp.exp2(mine - top), jnp.exp2(theirs - top)
        whole = weight_mine + weight_theirs
        result = acc_ref[i, :HEAD_DIM] * (weight_mine / (sums * whole)) + other_ref[
            i, :HEAD_DIM
        ].astype(F32) * (weight_theirs / whole)
        result = result.astype(BF16)
        for h in range(2):
            out_ref[i, :, h * HEAD_DIM : (h + 1) * HEAD_DIM] = result[
                :, h * BLOCK : (h + 1) * BLOCK
            ].T


def combine(state, other):
    return pl.pallas_call(
        combine_kernel,
        out_shape=jax.ShapeDtypeStruct((BLOCKS, BLOCK, 2 * HEAD_DIM), BF16),
        in_specs=[VMEM] * 3,
        out_specs=VMEM,
        name="combine",
    )(*state, other)


def body(queries, keys, values, block_order):
    rows = queries.shape[0]
    group = ("c", "yl", "x")
    z_size = lax.axis_size("z")
    meta = jnp.stack([lax.axis_index("yh"), lax.axis_index("z"), lax.axis_index("c")]).astype(jnp.int32)
    to_send = jnp.concatenate(
        [
            queries.reshape(rows, 8, 2, 256).transpose(2, 1, 0, 3),
            jnp.broadcast_to(keys.reshape(rows, 8, 128).transpose(1, 0, 2)[None], (2, 8, rows, 128)),
            jnp.broadcast_to(values.reshape(rows, 8, 128).transpose(1, 0, 2)[None], (2, 8, rows, 128)),
        ],
        axis=3,
    ).reshape(16, rows, 512)
    got = lax.all_to_all(to_send, group, 0, 0, tiled=True).reshape(BLOCKS, BLOCK, 512)
    q, kv = prepare(got)

    ring = [(2 * i + k, 2 * ((i + 1 - 2 * k) % z_size) + k) for i in range(z_size) for k in (0, 1)]
    swap = [(0, 1), (1, 0)]

    def onward(a):
        return lax.ppermute(a, ("z", "c"), ring)

    def swapped(a):
        return lax.ppermute(a, "c", swap)

    r1 = onward(kv)
    other_q = lax.ppermute(q, "yh", swap)
    s1, r2 = swapped(r1), onward(r1)
    s2, r3 = swapped(r2), onward(r2)
    r4 = onward(lax.dynamic_slice_in_dim(r3, 2 * lax.axis_index("c"), 2, 0))
    s3, s4 = swapped(r3), swapped(r4)

    mine = own_start(meta, block_order, q, kv)
    mine = attend(meta, block_order, q, [(r1, 1, 0), (s1, -1, 0)], mine, False)
    theirs = attend(meta, block_order, other_q, [(kv, 0, 0), (r1, 1, 0), (s1, -1, 0), (r2, 2, 0), (s2, -2, 0)], None, False)
    mine = attend(meta, block_order, q, [(r2, 2, 0), (s2, -2, 0)], mine, False)
    late = [(r3, 3, 0), (s3, -3, 0), (r4, 4, 0), (s4, -4, 1)]
    sent = attend(meta, block_order, other_q, late, theirs, True)
    other = lax.ppermute(sent, "yh", swap)
    mine = attend(meta, block_order, q, late, mine, False)
    result = combine(mine, other).reshape(16, rows, 256)
    back = lax.all_to_all(result, group, 0, 0, tiled=True)
    return back.reshape(2, 8, rows, 256).transpose(2, 1, 0, 3).reshape(rows, 4096)


def solution(mesh):
    fine = Mesh(mesh.devices.reshape(2, 8, 2, 2, 4), AXES)
    spec = P(AXES, None)
    return jax.shard_map(
        body, mesh=fine, in_specs=(spec, spec, spec, P()), out_specs=spec, check_vma=False
    )
```

```python
import functools

import jax
import jax.numpy as jnp
import numpy as np
from jax import lax
from jax.experimental import pallas as pl
from jax.experimental.pallas import tpu as pltpu
from jax.sharding import Mesh
from jax.sharding import PartitionSpec as P

HEAD_DIM = 128
BLOCK = 256
ROWS = 2 * BLOCK
BLOCKS = 4
EXTENDED = HEAD_DIM + 8
PARTIAL = HEAD_DIM + 16
NEG = -1e30
LOG2E_SCALE = float(np.log2(np.e) / np.sqrt(HEAD_DIM))
AXES = ("yh", "z", "c", "yl", "x")
F32 = jnp.float32
BF16 = jnp.bfloat16
SMEM = pl.BlockSpec(memory_space=pltpu.SMEM)
VMEM = pl.BlockSpec(memory_space=pltpu.VMEM)
VMEM_BYTES = 16 * 2**20
SMALL = pltpu.CompilerParams(vmem_limit_bytes=8 * 2**20)


def nt(a, b):
    return lax.dot_general(a, b, (((1,), (0,)), ((), ())), preferred_element_type=F32)


def prepare_kernel(got_ref, q_ref, kv_ref):
    for b in range(BLOCKS):
        for h in range(2):
            q_ref[b, :, h * BLOCK : (h + 1) * BLOCK] = got_ref[
                b, :, h * HEAD_DIM : (h + 1) * HEAD_DIM
            ].T
        kv_ref[b, :BLOCK] = got_ref[b, :, 2 * HEAD_DIM : 3 * HEAD_DIM]
        value = got_ref[b, :, 3 * HEAD_DIM :].T
        kv_ref[b, BLOCK : BLOCK + HEAD_DIM] = value[:, :HEAD_DIM]
        kv_ref[b, BLOCK + HEAD_DIM :] = value[:, HEAD_DIM:]


def prepare(got):
    return pl.pallas_call(
        prepare_kernel,
        out_shape=(
            jax.ShapeDtypeStruct((BLOCKS, HEAD_DIM, ROWS), BF16),
            jax.ShapeDtypeStruct((BLOCKS, 2 * BLOCK, HEAD_DIM), BF16),
        ),
        in_specs=[VMEM],
        out_specs=(VMEM, VMEM),
        compiler_params=SMALL,
        name="prepare",
    )(got)


def value_of(kv_ref, t):
    return jnp.concatenate(
        [kv_ref[t, BLOCK : BLOCK + HEAD_DIM], kv_ref[t, BLOCK + HEAD_DIM :]], axis=1
    )


def own_kernel(meta_ref, order_ref, q_ref, kv_ref, m_ref, acc_ref):
    first = (meta_ref[0] * 8 + meta_ref[1]) * BLOCKS
    values = jnp.concatenate([value_of(kv_ref, t) for t in range(BLOCKS)], axis=1)
    lhs = jnp.concatenate([values, jnp.ones((16, BLOCKS * BLOCK), BF16)], axis=0)
    keys = jnp.concatenate([kv_ref[t, :BLOCK] for t in range(BLOCKS)], axis=0)
    row = lax.broadcasted_iota(jnp.int32, (BLOCK, ROWS), 0)
    col = lax.broadcasted_iota(jnp.int32, (BLOCK, ROWS), 1) & (BLOCK - 1)
    ahead = row - col
    for i in range(BLOCKS):
        scores = nt(keys, q_ref[i]) * LOG2E_SCALE
        q_pos = order_ref[first + i] * BLOCK
        parts = []
        for t in range(BLOCKS):
            part = scores[t * BLOCK : (t + 1) * BLOCK]
            room = q_pos - order_ref[first + t] * BLOCK
            parts.append(jnp.where(ahead <= room, part, NEG))
        scores = jnp.concatenate(parts, axis=0)
        row_max = jnp.max(scores, axis=0, keepdims=True)
        m_ref[i] = row_max
        acc_ref[i] = nt(lhs, jnp.exp2(scores - row_max).astype(BF16))[:EXTENDED]


def own_start(meta, order, q, kv):
    return pl.pallas_call(
        own_kernel,
        out_shape=(
            jax.ShapeDtypeStruct((BLOCKS, 1, ROWS), F32),
            jax.ShapeDtypeStruct((BLOCKS, EXTENDED, ROWS), F32),
        ),
        in_specs=[SMEM, SMEM, VMEM, VMEM],
        out_specs=(VMEM, VMEM),
        compiler_params=pltpu.CompilerParams(vmem_limit_bytes=VMEM_BYTES),
        cost_estimate=pl.CostEstimate(
            flops=16 * 4 * BLOCK * ROWS * 8, bytes_accessed=1 << 18, transcendentals=1 << 16
        ),
        name="own_start",
    )(meta, order, q, kv)


def attend_kernel(steps, partner, starts, final, *refs):
    count = len(steps)
    meta_ref, order_ref = refs[:2]
    q_refs, refs = (refs[2:4], refs[4:]) if partner else (refs[2:3], refs[3:])
    kv_refs = refs[:count]
    rest = refs[count:]
    if not starts:
        m_in, acc_in = rest[:2]
        rest = rest[2:]
    if final:
        out_ref, rest = rest[0], rest[1:]
    m_ref, acc_ref, kv_s, scores_a, scores_b, max_a, max_b = rest[:7]
    item_q, item_k, item_v, item_f = rest[7:11]
    if partner:
        q_ref = rest[11]
        for n in range(2):
            q_ref[2 * n : 2 * n + 2] = q_refs[n][...]
    else:
        q_ref = q_refs[0]

    total = sum(size for size, _, _ in steps)
    if starts:
        m_ref[...] = jnp.full(m_ref.shape, NEG, F32)
        acc_ref[...] = jnp.zeros(acc_ref.shape, F32)
    else:
        m_ref[...] = m_in[...]
        acc_ref[...] = acc_in[...]
    at = 0
    for n, (size, _, _) in enumerate(steps):
        kv_s[at : at + size] = kv_refs[n][...]
        at += size
    kv_s[total] = jnp.zeros((2 * BLOCK, HEAD_DIM), BF16)

    yh, z, c = meta_ref[0], meta_ref[1], meta_ref[2]
    up = 2 * c - 1
    q_first = ((1 - yh if partner else yh) * 8 + z) * BLOCKS
    k_pos = []
    for size, distance, half in steps:
        plane = (z + up * distance + 16) & 7
        base = (yh * 8 + plane) * BLOCKS
        if size < BLOCKS:
            base = base + (c if half == 0 else 1 - c) * size
        k_pos.extend(order_ref[base + b] for b in range(size))

    begin = 0
    for i in range(BLOCKS):
        q_pos = order_ref[q_first + i]
        fill = begin
        for t in range(total):
            item_q[fill >> 1] = i
            item_k[fill] = t
            item_v[fill] = t
            item_f[fill] = 1.0
            fill = fill + jnp.where(k_pos[t] < q_pos, 1, 0)
        last = item_k[jnp.maximum(fill - 1, 0)]
        item_k[fill] = last
        item_v[fill] = total
        item_f[fill] = 0.0
        begin = begin + (((fill - begin) + 1) >> 1) * 2
    items = begin >> 1
    back = jnp.maximum(items - 1, 0)
    again_q = jnp.where(items > 0, item_q[back], 0)
    again_k = jnp.where(items > 0, item_k[2 * back], 0)
    again_l = jnp.where(items > 0, item_k[2 * back + 1], 0)
    for n in range(2):
        item_q[items + n] = again_q
        item_k[2 * (items + n)] = again_k
        item_k[2 * (items + n) + 1] = again_l
        item_v[2 * (items + n)] = total
        item_v[2 * (items + n) + 1] = total
        item_f[2 * (items + n)] = 0.0
        item_f[2 * (items + n) + 1] = 0.0

    halves = [slice(0, BLOCK), slice(BLOCK, ROWS)]

    def score(j, scores, maxima, cols):
        keys = jnp.concatenate([kv_s[item_k[2 * j], :BLOCK], kv_s[item_k[2 * j + 1], :BLOCK]], 0)
        s = nt(keys, q_ref[item_q[j], :, cols]) * LOG2E_SCALE
        scores[:, cols] = s
        maxima[:, cols] = jnp.max(s, axis=0, keepdims=True)

    def absorb(j, scores, maxima, cols):
        i = item_q[j]
        values = jnp.concatenate([value_of(kv_s, item_v[2 * j + n]) for n in range(2)], axis=1)
        ones = jnp.concatenate(
            [jnp.full((16, BLOCK), item_f[2 * j + n], F32).astype(BF16) for n in range(2)], axis=1
        )
        lhs = jnp.concatenate([values, ones], axis=0)
        old = m_ref[i, :, cols]
        new = jnp.maximum(old, maxima[:, cols])
        keep = jnp.exp2(old - new)
        m_ref[i, :, cols] = new
        p = jnp.exp2(scores[:, cols] - new).astype(BF16)
        acc_ref[i, :, cols] = acc_ref[i, :, cols] * keep + nt(lhs, p)[:EXTENDED]

    def both(j, scores, maxima, next_scores, next_maxima):
        for cols in halves:
            score(j + 1, next_scores, next_maxima, cols)
            absorb(j, scores, maxima, cols)

    def several(at_once, first):
        def turn(h, carry):
            j = first + at_once * h
            for n in range(0, at_once, 2):
                both(j + n, scores_a, max_a, scores_b, max_b)
                both(j + n + 1, scores_b, max_b, scores_a, max_a)
            return carry

        return turn

    for cols in halves:
        score(0, scores_a, max_a, cols)
    fours = items >> 2
    lax.fori_loop(0, fours, several(4, 0), 0)
    lax.fori_loop(0, (items - 4 * fours + 1) >> 1, several(2, 4 * fours), 0)

    if final:
        sub = lax.broadcasted_iota(jnp.int32, (16, ROWS), 0)
        for i in range(BLOCKS):
            sums = acc_ref[i, HEAD_DIM : HEAD_DIM + 1]
            some = sums > 0.0
            safe = jnp.where(some, sums, 1.0)
            logs = jnp.where(some, m_ref[i] + jnp.log2(safe), NEG)
            high = logs.astype(BF16).astype(F32)
            middle = (logs - high).astype(BF16).astype(F32)
            low = logs - high - middle
            out_ref[i, :HEAD_DIM] = (acc_ref[i, :HEAD_DIM] * (1.0 / safe)).astype(BF16)
            out_ref[i, HEAD_DIM:] = jnp.where(
                sub == 0, high, jnp.where(sub == 1, middle, jnp.where(sub == 2, low, 0.0))
            ).astype(BF16)


def attend(meta, order, q, shards, state, partner, final):
    steps = tuple((a.shape[0], distance, half) for a, distance, half in shards)
    total = sum(s[0] for s in steps)
    starts = state is None
    args = [meta, order] + list(q) + [a for a, _, _ in shards] + ([] if starts else list(state))
    m_shape, acc_shape = (BLOCKS, 1, ROWS), (BLOCKS, EXTENDED, ROWS)
    if final:
        out_shape = (jax.ShapeDtypeStruct((BLOCKS, PARTIAL, ROWS), BF16),)
        work = [pltpu.VMEM(m_shape, F32), pltpu.VMEM(acc_shape, F32)]
    else:
        out_shape = (jax.ShapeDtypeStruct(m_shape, F32), jax.ShapeDtypeStruct(acc_shape, F32))
        work = []
    pairs = BLOCKS * total // 2
    slots = 2 * (BLOCKS * ((total + 1) // 2) + 4)
    got = pl.pallas_call(
        functools.partial(attend_kernel, steps, partner, starts, final),
        out_shape=out_shape,
        in_specs=[SMEM, SMEM] + [VMEM] * (len(args) - 2),
        out_specs=tuple(VMEM for _ in out_shape),
        scratch_shapes=work
        + [
            pltpu.VMEM((total + 1, 2 * BLOCK, HEAD_DIM), BF16),
            pltpu.VMEM((2 * BLOCK, ROWS), F32),
            pltpu.VMEM((2 * BLOCK, ROWS), F32),
            pltpu.VMEM((1, ROWS), F32),
            pltpu.VMEM((1, ROWS), F32),
            pltpu.SMEM((slots // 2,), jnp.int32),
            pltpu.SMEM((slots,), jnp.int32),
            pltpu.SMEM((slots,), jnp.int32),
            pltpu.SMEM((slots,), F32),
        ]
        + ([pltpu.VMEM((BLOCKS, HEAD_DIM, ROWS), BF16)] if partner else []),
        compiler_params=pltpu.CompilerParams(vmem_limit_bytes=VMEM_BYTES),
        cost_estimate=pl.CostEstimate(
            flops=pairs * 4 * BLOCK * ROWS * 8,
            bytes_accessed=1 << 18,
            transcendentals=pairs * BLOCK * ROWS // 32,
        ),
        name="attend",
    )(*args)
    return got[0] if final else got


def combine_kernel(m_ref, acc_ref, other_ref, out_ref):
    for i in range(BLOCKS):
        sums = acc_ref[i, HEAD_DIM : HEAD_DIM + 1]
        mine = m_ref[i] + jnp.log2(sums)
        tail = other_ref[i, HEAD_DIM:].astype(F32)
        theirs = tail[0:1] + tail[1:2] + tail[2:3]
        top = jnp.maximum(mine, theirs)
        weight_mine, weight_theirs = jnp.exp2(mine - top), jnp.exp2(theirs - top)
        whole = weight_mine + weight_theirs
        result = acc_ref[i, :HEAD_DIM] * (weight_mine / (sums * whole)) + other_ref[
            i, :HEAD_DIM
        ].astype(F32) * (weight_theirs / whole)
        result = result.astype(BF16)
        for h in range(2):
            out_ref[i, :, h * HEAD_DIM : (h + 1) * HEAD_DIM] = result[
                :, h * BLOCK : (h + 1) * BLOCK
            ].T


def combine(state, other):
    return pl.pallas_call(
        combine_kernel,
        out_shape=jax.ShapeDtypeStruct((BLOCKS, BLOCK, 2 * HEAD_DIM), BF16),
        in_specs=[VMEM] * 3,
        out_specs=VMEM,
        compiler_params=SMALL,
        name="combine",
    )(*state, other)


def pack_kernel(queries_ref, keys_ref, values_ref, out_ref):
    for g in range(8):
        keys = keys_ref[:, g * HEAD_DIM : (g + 1) * HEAD_DIM]
        values = values_ref[:, g * HEAD_DIM : (g + 1) * HEAD_DIM]
        for c in range(2):
            first = (2 * g + c) * 2 * HEAD_DIM
            out_ref[8 * c + g, :, : 2 * HEAD_DIM] = queries_ref[:, first : first + 2 * HEAD_DIM]
            out_ref[8 * c + g, :, 2 * HEAD_DIM : 3 * HEAD_DIM] = keys
            out_ref[8 * c + g, :, 3 * HEAD_DIM :] = values


def pack(queries, keys, values):
    rows = queries.shape[0]
    return pl.pallas_call(
        pack_kernel,
        out_shape=jax.ShapeDtypeStruct((16, rows, 4 * HEAD_DIM), BF16),
        in_specs=[VMEM] * 3,
        out_specs=VMEM,
        compiler_params=SMALL,
        name="pack",
    )(queries, keys, values)


def unpack_kernel(back_ref, out_ref):
    for g in range(8):
        for c in range(2):
            first = (2 * g + c) * 2 * HEAD_DIM
            out_ref[:, first : first + 2 * HEAD_DIM] = back_ref[8 * c + g]


def unpack(back):
    rows = back.shape[1]
    return pl.pallas_call(
        unpack_kernel,
        out_shape=jax.ShapeDtypeStruct((rows, 32 * HEAD_DIM), BF16),
        in_specs=[VMEM],
        out_specs=VMEM,
        compiler_params=SMALL,
        name="unpack",
    )(back)


def body(queries, keys, values, block_order):
    rows = queries.shape[0]
    group = ("c", "yl", "x")
    z_size = lax.axis_size("z")
    meta = jnp.stack([lax.axis_index("yh"), lax.axis_index("z"), lax.axis_index("c")]).astype(jnp.int32)
    got = lax.all_to_all(pack(queries, keys, values), group, 0, 0, tiled=True)
    q, kv = prepare(got.reshape(BLOCKS, BLOCK, 512))

    ring = [(2 * i + k, 2 * ((i + 1 - 2 * k) % z_size) + k) for i in range(z_size) for k in (0, 1)]
    swap = [(0, 1), (1, 0)]

    def onward(a):
        return lax.ppermute(a, ("z", "c"), ring)

    def swapped(a):
        return lax.ppermute(a, "c", swap)

    r1 = onward(kv)
    other_a = lax.ppermute(q[:2], "yh", swap)
    mine = own_start(meta, block_order, q, kv)
    r1, mine, other_a, q = lax.optimization_barrier((r1, mine, other_a, q))

    r2, s1 = onward(r1), swapped(r1)
    other_q = (other_a, lax.ppermute(q[2:], "yh", swap))
    near = [(r1, 1, 0), (s1, -1, 0)]
    mine = attend(meta, block_order, (q,), near, mine, False, False)
    r2, mine, other_q = lax.optimization_barrier((r2, mine, other_q))

    r3, s2 = onward(r2), swapped(r2)
    theirs = attend(meta, block_order, other_q, [(kv, 0, 0)] + near, None, True, False)
    r3, theirs = lax.optimization_barrier((r3, theirs))

    r4 = onward(lax.dynamic_slice_in_dim(r3, 2 * lax.axis_index("c"), 2, 0))
    s3 = swapped(r3)
    middle = [(r2, 2, 0), (s2, -2, 0)]
    theirs = attend(meta, block_order, other_q, middle, theirs, True, False)
    r4, theirs = lax.optimization_barrier((r4, theirs))

    s4 = swapped(r4)
    far = [(r3, 3, 0), (s3, -3, 0), (r4, 4, 0), (s4, -4, 1)]
    sent = attend(meta, block_order, other_q, far, theirs, True, True)
    other = lax.ppermute(sent, "yh", swap)
    mine = attend(meta, block_order, (q,), middle + far, mine, False, False)
    result = combine(mine, other).reshape(16, rows, 256)
    return unpack(lax.all_to_all(result, group, 0, 0, tiled=True))


def solution(mesh):
    fine = Mesh(mesh.devices.reshape(2, 8, 2, 2, 4), AXES)
    spec = P(AXES, None)
    return jax.shard_map(
        body, mesh=fine, in_specs=(spec, spec, spec, P()), out_specs=spec, check_vma=False
    )
```

```python
import functools

import jax
import jax.numpy as jnp
import numpy as np
from jax import lax
from jax.experimental import pallas as pl
from jax.experimental.pallas import tpu as pltpu
from jax.sharding import Mesh
from jax.sharding import PartitionSpec as P

HEAD_DIM = 128
HALF = 128
ROWS = 2 * HALF
BLOCKS = 8
GROUP = 4
EXTENDED = HEAD_DIM + 8
PARTIAL = BLOCKS * HEAD_DIM
NEG = -1e30
LOG2E_SCALE = float(np.log2(np.e) / np.sqrt(HEAD_DIM))
AXES = ("yh", "z", "c", "yl", "x")
F32 = jnp.float32
BF16 = jnp.bfloat16
SMEM = pl.BlockSpec(memory_space=pltpu.SMEM)
VMEM = pl.BlockSpec(memory_space=pltpu.VMEM)
VMEM_BYTES = 16 * 2**20
SMALL = pltpu.CompilerParams(vmem_limit_bytes=8 * 2**20)


def nt(a, b):
    return lax.dot_general(a, b, (((1,), (0,)), ((), ())), preferred_element_type=F32)


def prepare_kernel(got_ref, q_ref, kv_ref):
    for b in range(BLOCKS):
        for h in range(2):
            q_ref[b, :, h * HALF : (h + 1) * HALF] = got_ref[
                b, :, h * HEAD_DIM : (h + 1) * HEAD_DIM
            ].T
        kv_ref[b, :HALF] = got_ref[b, :, 2 * HEAD_DIM : 3 * HEAD_DIM]
        kv_ref[b, HALF:] = got_ref[b, :, 3 * HEAD_DIM :].T


def prepare(got):
    return pl.pallas_call(
        prepare_kernel,
        out_shape=(
            jax.ShapeDtypeStruct((BLOCKS, HEAD_DIM, ROWS), BF16),
            jax.ShapeDtypeStruct((BLOCKS, 2 * HALF, HEAD_DIM), BF16),
        ),
        in_specs=[VMEM],
        out_specs=(VMEM, VMEM),
        compiler_params=SMALL,
        name="prepare",
    )(got)


def attend_kernel(steps, partner, starts, final, *refs):
    shards = len(steps)
    meta_ref, order_ref = refs[:2]
    q_refs, refs = (refs[2:4], refs[4:]) if partner else (refs[2:3], refs[3:])
    kv_refs = refs[:shards]
    rest = refs[shards:]
    if not starts:
        m_in, acc_in = rest[:2]
        rest = rest[2:]
    if final:
        out_ref, rest = rest[0], rest[1:]
    m_ref, acc_ref, kv_s = rest[:3]
    scores, maxima = rest[3:7], rest[7:11]
    item, slots, before, sorted_k = rest[11:15]
    if partner:
        q_ref = rest[15]
        split = q_refs[0].shape[0]
        q_ref[:split] = q_refs[0][...]
        q_ref[split:] = q_refs[1][...]
    else:
        q_ref = q_refs[0]

    total = BLOCKS * shards
    for n in range(shards):
        kv_s[n * BLOCKS : (n + 1) * BLOCKS] = kv_refs[n][...]
    kv_s[total] = jnp.zeros((2 * HALF, HEAD_DIM), BF16)

    yh, z, c = meta_ref[0], meta_ref[1], meta_ref[2]
    up = 2 * c - 1
    q_pos = [order_ref[((i // 4) * 8 + z) * 4 + i % 4] for i in range(BLOCKS)]
    k_pos = []
    for distance in steps:
        plane = (z + up * distance + 16) & 7
        k_pos += [order_ref[((b // 4) * 8 + plane) * 4 + b % 4] for b in range(BLOCKS)]

    for p in range(64):
        slots[p] = -1
    for t in range(total):
        slots[k_pos[t]] = t
    count = 0
    for p in range(64):
        found = slots[p]
        sorted_k[count] = found
        before[p] = count
        count = count + jnp.where(found >= 0, 1, 0)

    items = 0
    code = 0
    for i in range(BLOCKS):
        n_seen = before[q_pos[i]]
        mine = (i << 16) | (n_seen << 8)
        for n in range((total + GROUP - 1) // GROUP):
            item[items + n] = mine | (GROUP * n)
        code = jnp.where(n_seen > 0, mine | n_seen, code)
        items = items + ((n_seen + GROUP - 1) >> 2)
    for n in range(5):
        item[items + n] = code

    if starts:
        key_at = lax.broadcasted_iota(jnp.int32, (HALF, ROWS), 0)
        row_at = lax.broadcasted_iota(jnp.int32, (HALF, ROWS), 1) & (HALF - 1)
        key_side, row_side = yh, 1 - yh if partner else yh
        key_at = (key_at >> 5) * 64 + key_side * 32 + (key_at & 31)
        row_at = (row_at >> 5) * 64 + row_side * 32 + (row_at & 31)
        seen = key_at <= row_at
        ones = jnp.ones((16, HALF), BF16)
        for i in range(BLOCKS):
            s = jnp.where(seen, nt(kv_s[i, :HALF], q_ref[i]) * LOG2E_SCALE, NEG)
            top = jnp.max(s, axis=0, keepdims=True)
            p = jnp.where(seen, jnp.exp2(s - top), 0.0).astype(BF16)
            m_ref[i] = top
            acc_ref[i] = nt(jnp.concatenate([kv_s[i, HALF:], ones], axis=0), p)[:EXTENDED]
    else:
        m_ref[...] = m_in[...]
        acc_ref[...] = acc_in[...]

    def places(j):
        code = item[j]
        seen_count, base = (code >> 8) & 255, code & 255
        at = [base + g for g in range(GROUP)]
        blocks = [sorted_k[jnp.maximum(jnp.minimum(n, seen_count - 1), 0)] for n in at]
        return code >> 16, blocks, [n < seen_count for n in at]

    def score(j, scores, maxima):
        i, blocks, _ = places(j)
        keys = jnp.concatenate([kv_s[t, :HALF] for t in blocks], axis=0)
        s = nt(keys, q_ref[i]) * LOG2E_SCALE
        scores[...] = s
        maxima[...] = jnp.max(s, axis=0, keepdims=True)

    def absorb(j, scores, maxima):
        i, blocks, counts = places(j)
        values = [kv_s[jnp.where(ok, t, total), HALF:] for t, ok in zip(blocks, counts)]
        ones = [jnp.full((16, HALF), jnp.where(ok, 1.0, 0.0), F32).astype(BF16) for ok in counts]
        lhs = jnp.concatenate([jnp.concatenate(values, axis=1), jnp.concatenate(ones, axis=1)], axis=0)
        old = m_ref[i]
        new = jnp.maximum(old, maxima[...])
        keep = jnp.exp2(old - new)
        m_ref[i] = new
        p = jnp.exp2(scores[...] - new).astype(BF16)
        acc_ref[i] = acc_ref[i] * keep + nt(lhs, p)[:EXTENDED]

    def several(at_once, first):
        def turn(h, carry):
            j = first + at_once * h
            for n in range(at_once):
                score(j + n + 2, scores[(n + 2) % 4], maxima[(n + 2) % 4])
                absorb(j + n, scores[n % 4], maxima[n % 4])
            return carry

        return turn

    for n in range(2):
        score(n, scores[n], maxima[n])
    many = items >> 3
    lax.fori_loop(0, many, several(8, 0), 0)
    lax.fori_loop(0, (items - 8 * many + 3) >> 2, several(4, 8 * many), 0)

    if final:
        sub = lax.broadcasted_iota(jnp.int32, (32, ROWS), 0)
        tail = jnp.zeros((32, ROWS), F32)
        for i in range(BLOCKS):
            sums = acc_ref[i, HEAD_DIM : HEAD_DIM + 1]
            some = sums > 0.0
            safe = jnp.where(some, sums, 1.0)
            logs = jnp.where(some, m_ref[i] + jnp.log2(safe), NEG)
            high = logs.astype(BF16).astype(F32)
            middle = (logs - high).astype(BF16).astype(F32)
            low = logs - high - middle
            out_ref[i * HEAD_DIM : (i + 1) * HEAD_DIM] = (
                acc_ref[i, :HEAD_DIM] * (1.0 / safe)
            ).astype(BF16)
            for n, part in enumerate((high, middle, low)):
                tail = jnp.where(sub == BLOCKS * n + i, part, tail)
        out_ref[PARTIAL:] = tail.astype(BF16)


def attend(meta, order, q, shards, state, partner, final=False):
    steps = tuple(distance for _, distance in shards)
    total = BLOCKS * len(steps)
    starts = state is None
    args = [meta, order] + list(q) + [a for a, _ in shards] + ([] if starts else list(state))
    m_shape, acc_shape = (BLOCKS, 1, ROWS), (BLOCKS, EXTENDED, ROWS)
    if final:
        out_shape = (jax.ShapeDtypeStruct((PARTIAL + 32, ROWS), BF16),)
        work = [pltpu.VMEM(m_shape, F32), pltpu.VMEM(acc_shape, F32)]
    else:
        out_shape = (jax.ShapeDtypeStruct(m_shape, F32), jax.ShapeDtypeStruct(acc_shape, F32))
        work = []
    pairs = BLOCKS * total // 2
    items = BLOCKS * ((total + GROUP - 1) // GROUP) + 8
    got = pl.pallas_call(
        functools.partial(attend_kernel, steps, partner, starts, final),
        out_shape=out_shape,
        in_specs=[SMEM, SMEM] + [VMEM] * (len(args) - 2),
        out_specs=tuple(VMEM for _ in out_shape),
        scratch_shapes=work
        + [
            pltpu.VMEM((total + 1, 2 * HALF, HEAD_DIM), BF16),
        ]
        + [pltpu.VMEM((GROUP * HALF, ROWS), F32)] * 4
        + [pltpu.VMEM((1, ROWS), F32)] * 4
        + [
            pltpu.SMEM((items,), jnp.int32),
            pltpu.SMEM((64,), jnp.int32),
            pltpu.SMEM((64,), jnp.int32),
            pltpu.SMEM((total + 1,), jnp.int32),
        ]
        + ([pltpu.VMEM((BLOCKS, HEAD_DIM, ROWS), BF16)] if partner else []),
        compiler_params=pltpu.CompilerParams(vmem_limit_bytes=VMEM_BYTES),
        cost_estimate=pl.CostEstimate(
            flops=pairs * 4 * HALF * ROWS * 8, bytes_accessed=1 << 18, transcendentals=pairs * 1024
        ),
        name="attend",
    )(*args)
    return got[0] if final else got


def combine_kernel(m_ref, acc_ref, other_ref, out_ref):
    tail = other_ref[PARTIAL:].astype(F32)
    logs = tail[:BLOCKS] + tail[BLOCKS : 2 * BLOCKS] + tail[2 * BLOCKS : 3 * BLOCKS]
    for i in range(BLOCKS):
        sums = acc_ref[i, HEAD_DIM : HEAD_DIM + 1]
        mine = m_ref[i] + jnp.log2(sums)
        theirs = logs[i : i + 1]
        top = jnp.maximum(mine, theirs)
        weight_mine, weight_theirs = jnp.exp2(mine - top), jnp.exp2(theirs - top)
        whole = weight_mine + weight_theirs
        result = acc_ref[i, :HEAD_DIM] * (weight_mine / (sums * whole)) + other_ref[
            i * HEAD_DIM : (i + 1) * HEAD_DIM
        ].astype(F32) * (weight_theirs / whole)
        result = result.astype(BF16)
        for h in range(2):
            out_ref[i, :, h * HEAD_DIM : (h + 1) * HEAD_DIM] = result[
                :, h * HALF : (h + 1) * HALF
            ].T


def combine(state, other):
    return pl.pallas_call(
        combine_kernel,
        out_shape=jax.ShapeDtypeStruct((BLOCKS, HALF, 2 * HEAD_DIM), BF16),
        in_specs=[VMEM] * 3,
        out_specs=VMEM,
        compiler_params=SMALL,
        name="combine",
    )(*state, other)


def pack_kernel(queries_in, keys_in, values_in, out_ref, queries_ref, keys_ref, values_ref, sems):
    pairs = ((queries_in, queries_ref), (keys_in, keys_ref), (values_in, values_ref))
    copies = [pltpu.make_async_copy(a, b, sems.at[n]) for n, (a, b) in enumerate(pairs)]
    for copy in copies:
        copy.start()
    for copy in copies:
        copy.wait()
    rows = out_ref.shape[1]
    for side in range(2):
        part = slice(side * rows, (side + 1) * rows)
        for g in range(8):
            keys = keys_ref[part, g * HEAD_DIM : (g + 1) * HEAD_DIM]
            values = values_ref[part, g * HEAD_DIM : (g + 1) * HEAD_DIM]
            for c in range(2):
                first = (2 * g + c) * 2 * HEAD_DIM
                at = 16 * side + 8 * c + g
                out_ref[at, :, : 2 * HEAD_DIM] = queries_ref[part, first : first + 2 * HEAD_DIM]
                out_ref[at, :, 2 * HEAD_DIM : 3 * HEAD_DIM] = keys
                out_ref[at, :, 3 * HEAD_DIM :] = values


def pack(queries, keys, values):
    rows = queries.shape[0]
    return pl.pallas_call(
        pack_kernel,
        out_shape=jax.ShapeDtypeStruct((32, rows // 2, 4 * HEAD_DIM), BF16),
        in_specs=[pl.BlockSpec(memory_space=pl.ANY)] * 3,
        out_specs=VMEM,
        scratch_shapes=[pltpu.VMEM(a.shape, BF16) for a in (queries, keys, values)]
        + [pltpu.SemaphoreType.DMA((3,))],
        compiler_params=pltpu.CompilerParams(vmem_limit_bytes=56 * 2**20),
        name="pack",
    )(queries, keys, values)


def unpack_kernel(back_ref, out_ref):
    rows = back_ref.shape[1]
    for side in range(2):
        for g in range(8):
            for c in range(2):
                first = (2 * g + c) * 2 * HEAD_DIM
                out_ref[side * rows : (side + 1) * rows, first : first + 2 * HEAD_DIM] = back_ref[
                    16 * side + 8 * c + g
                ]


def unpack(back):
    rows = 2 * back.shape[1]
    return pl.pallas_call(
        unpack_kernel,
        out_shape=jax.ShapeDtypeStruct((rows, 32 * HEAD_DIM), BF16),
        in_specs=[VMEM],
        out_specs=VMEM,
        compiler_params=SMALL,
        name="unpack",
    )(back)


def body(queries, keys, values, block_order):
    rows = queries.shape[0]
    group = ("yh", "c", "yl", "x")
    z_size = lax.axis_size("z")
    meta = jnp.stack([lax.axis_index("yh"), lax.axis_index("z"), lax.axis_index("c")]).astype(jnp.int32)
    got = lax.all_to_all(pack(queries, keys, values), group, 0, 0, tiled=True)
    q, kv = prepare(got.reshape(BLOCKS, HALF, 512))

    ring = [(2 * i + k, 2 * ((i + 1 - 2 * k) % z_size) + k) for i in range(z_size) for k in (0, 1)]
    swap = [(0, 1), (1, 0)]

    def onward(a):
        return lax.ppermute(a, ("z", "c"), ring)

    def swapped(a):
        return lax.ppermute(a, "c", swap)

    r1 = onward(kv)
    other_a = lax.ppermute(q[:5], "yh", swap)
    mine = attend(meta, block_order, (q,), [(kv, 0)], None, False)
    r1, mine, other_a, q = lax.optimization_barrier((r1, mine, other_a, q))

    r2, s1 = onward(r1), swapped(r1)
    other_q = (other_a, lax.ppermute(q[5:], "yh", swap))
    near = [(r1, 1), (s1, -1)]
    r2, other_q = lax.optimization_barrier((r2, other_q))

    r3, s2 = onward(r2), swapped(r2)
    theirs = attend(meta, block_order, other_q, [(kv, 0)] + near, None, True)
    r3, theirs = lax.optimization_barrier((r3, theirs))

    r4, s3 = onward(r3), swapped(r3)
    later = [(r2, 2), (s2, -2), (r3, 3), (s3, -3)]
    theirs = attend(meta, block_order, other_q, later, theirs, True)
    r4, theirs = lax.optimization_barrier((r4, theirs))

    last = [(r4, 4)]
    sent = attend(meta, block_order, other_q, last, theirs, True, True)
    other = lax.ppermute(sent, "yh", swap)
    mine = attend(meta, block_order, (q,), near + later + last, mine, False)
    result = combine(mine, other).reshape(32, rows // 2, 256)
    return unpack(lax.all_to_all(result, group, 0, 0, tiled=True))


def solution(mesh):
    fine = Mesh(mesh.devices.reshape(2, 8, 2, 2, 4), AXES)
    spec = P(AXES, None)
    return jax.shard_map(
        body, mesh=fine, in_specs=(spec, spec, spec, P()), out_specs=spec, check_vma=False
    )
```

```python
import functools

import jax
import jax.numpy as jnp
import numpy as np
from jax import lax
from jax.experimental import pallas as pl
from jax.experimental.pallas import tpu as pltpu
from jax.sharding import Mesh
from jax.sharding import PartitionSpec as P

HEAD_DIM = 128
BLOCK = 256
ROWS = 2 * BLOCK
BLOCKS = 4
EXTENDED = HEAD_DIM + 8
GROUP = 2
PARTIAL = BLOCKS * HEAD_DIM
NEG = -1e30
LOG2E_SCALE = float(np.log2(np.e) / np.sqrt(HEAD_DIM))
AXES = ("yh", "z", "c", "yl", "x")
F32 = jnp.float32
BF16 = jnp.bfloat16
SMEM = pl.BlockSpec(memory_space=pltpu.SMEM)
VMEM = pl.BlockSpec(memory_space=pltpu.VMEM)
VMEM_BYTES = 16 * 2**20
SMALL = pltpu.CompilerParams(vmem_limit_bytes=8 * 2**20)


def nt(a, b):
    return lax.dot_general(a, b, (((1,), (0,)), ((), ())), preferred_element_type=F32)


def prepare_kernel(got_ref, q_ref, kv_ref):
    for b in range(BLOCKS):
        for h in range(2):
            q_ref[b, :, h * BLOCK : (h + 1) * BLOCK] = got_ref[
                b, :, h * HEAD_DIM : (h + 1) * HEAD_DIM
            ].T
        kv_ref[b, :BLOCK] = got_ref[b, :, 2 * HEAD_DIM : 3 * HEAD_DIM]
        value = got_ref[b, :, 3 * HEAD_DIM :].T
        kv_ref[b, BLOCK : BLOCK + HEAD_DIM] = value[:, :HEAD_DIM]
        kv_ref[b, BLOCK + HEAD_DIM :] = value[:, HEAD_DIM:]


def prepare(got):
    return pl.pallas_call(
        prepare_kernel,
        out_shape=(
            jax.ShapeDtypeStruct((BLOCKS, HEAD_DIM, ROWS), BF16),
            jax.ShapeDtypeStruct((BLOCKS, 2 * BLOCK, HEAD_DIM), BF16),
        ),
        in_specs=[VMEM],
        out_specs=(VMEM, VMEM),
        compiler_params=SMALL,
        name="prepare",
    )(got)


def value_of(kv_ref, t):
    return jnp.concatenate(
        [kv_ref[t, BLOCK : BLOCK + HEAD_DIM], kv_ref[t, BLOCK + HEAD_DIM :]], axis=1
    )


def own_kernel(meta_ref, order_ref, q_ref, kv_ref, m_ref, acc_ref):
    first = (meta_ref[0] * 8 + meta_ref[1]) * BLOCKS
    values = jnp.concatenate([value_of(kv_ref, t) for t in range(BLOCKS)], axis=1)
    lhs = jnp.concatenate([values, jnp.ones((16, BLOCKS * BLOCK), BF16)], axis=0)
    keys = jnp.concatenate([kv_ref[t, :BLOCK] for t in range(BLOCKS)], axis=0)
    row = lax.broadcasted_iota(jnp.int32, (BLOCK, ROWS), 0)
    col = lax.broadcasted_iota(jnp.int32, (BLOCK, ROWS), 1) & (BLOCK - 1)
    ahead = row - col
    for i in range(BLOCKS):
        scores = nt(keys, q_ref[i]) * LOG2E_SCALE
        q_pos = order_ref[first + i] * BLOCK
        parts = []
        for t in range(BLOCKS):
            part = scores[t * BLOCK : (t + 1) * BLOCK]
            room = q_pos - order_ref[first + t] * BLOCK
            parts.append(jnp.where(ahead <= room, part, NEG))
        scores = jnp.concatenate(parts, axis=0)
        row_max = jnp.max(scores, axis=0, keepdims=True)
        m_ref[i] = row_max
        acc_ref[i] = nt(lhs, jnp.exp2(scores - row_max).astype(BF16))[:EXTENDED]


def own_start(meta, order, q, kv):
    return pl.pallas_call(
        own_kernel,
        out_shape=(
            jax.ShapeDtypeStruct((BLOCKS, 1, ROWS), F32),
            jax.ShapeDtypeStruct((BLOCKS, EXTENDED, ROWS), F32),
        ),
        in_specs=[SMEM, SMEM, VMEM, VMEM],
        out_specs=(VMEM, VMEM),
        compiler_params=pltpu.CompilerParams(vmem_limit_bytes=VMEM_BYTES),
        cost_estimate=pl.CostEstimate(
            flops=16 * 4 * BLOCK * ROWS * 8, bytes_accessed=1 << 18, transcendentals=1 << 16
        ),
        name="own_start",
    )(meta, order, q, kv)


def attend_kernel(steps, partner, starts, final, *refs):
    shards = len(steps)
    meta_ref, order_ref = refs[:2]
    q_refs, refs = (refs[2:4], refs[4:]) if partner else (refs[2:3], refs[3:])
    kv_refs = refs[:shards]
    rest = refs[shards:]
    if not starts:
        m_in, acc_in = rest[:2]
        rest = rest[2:]
    if final:
        out_ref, rest = rest[0], rest[1:]
    m_ref, acc_ref, kv_s, scores_a, scores_b, max_a, max_b = rest[:7]
    item, slots, before, sorted_k = rest[7:11]
    if partner:
        q_ref = rest[11]
        split = q_refs[0].shape[0]
        q_ref[:split] = q_refs[0][...]
        q_ref[split:] = q_refs[1][...]
    else:
        q_ref = q_refs[0]

    total = BLOCKS * shards
    for n in range(shards):
        kv_s[n * BLOCKS : (n + 1) * BLOCKS] = kv_refs[n][...]
    kv_s[total] = jnp.zeros((2 * BLOCK, HEAD_DIM), BF16)
    if starts:
        m_ref[...] = jnp.full(m_ref.shape, NEG, F32)
        acc_ref[...] = jnp.zeros(acc_ref.shape, F32)
    else:
        m_ref[...] = m_in[...]
        acc_ref[...] = acc_in[...]

    yh, z, c = meta_ref[0], meta_ref[1], meta_ref[2]
    up = 2 * c - 1
    q_side = 1 - yh if partner else yh
    q_pos = [order_ref[(q_side * 8 + z) * BLOCKS + i] for i in range(BLOCKS)]
    k_pos = []
    for distance in steps:
        plane = (z + up * distance + 16) & 7
        k_pos += [order_ref[(yh * 8 + plane) * BLOCKS + b] for b in range(BLOCKS)]

    for p in range(64):
        slots[p] = -1
    for t in range(total):
        slots[k_pos[t]] = t
    count = 0
    for p in range(64):
        found = slots[p]
        sorted_k[count] = found
        before[p] = count
        count = count + jnp.where(found >= 0, 1, 0)

    items = 0
    code = 0
    for i in range(BLOCKS):
        n_seen = before[q_pos[i]]
        mine = (i << 16) | (n_seen << 8)
        for n in range((total + GROUP - 1) // GROUP):
            item[items + n] = mine | (GROUP * n)
        code = jnp.where(n_seen > 0, mine | n_seen, code)
        items = items + ((n_seen + GROUP - 1) >> 1)
    for n in range(3):
        item[items + n] = code

    def places(j):
        code = item[j]
        seen_count, base = (code >> 8) & 255, code & 255
        at = [base + g for g in range(GROUP)]
        blocks = [sorted_k[jnp.maximum(jnp.minimum(n, seen_count - 1), 0)] for n in at]
        return code >> 16, blocks, [n < seen_count for n in at]

    halves = [slice(0, BLOCK), slice(BLOCK, ROWS)]

    def score(j, scores, maxima, cols):
        i, blocks, _ = places(j)
        keys = jnp.concatenate([kv_s[t, :BLOCK] for t in blocks], axis=0)
        s = nt(keys, q_ref[i, :, cols]) * LOG2E_SCALE
        scores[:, cols] = s
        maxima[:, cols] = jnp.max(s, axis=0, keepdims=True)

    def absorb(j, scores, maxima, cols):
        i, blocks, counts = places(j)
        values = [value_of(kv_s, jnp.where(ok, t, total)) for t, ok in zip(blocks, counts)]
        ones = [jnp.full((16, BLOCK), jnp.where(ok, 1.0, 0.0), F32).astype(BF16) for ok in counts]
        lhs = jnp.concatenate([jnp.concatenate(values, axis=1), jnp.concatenate(ones, axis=1)], axis=0)
        old = m_ref[i, :, cols]
        new = jnp.maximum(old, maxima[:, cols])
        keep = jnp.exp2(old - new)
        m_ref[i, :, cols] = new
        p = jnp.exp2(scores[:, cols] - new).astype(BF16)
        acc_ref[i, :, cols] = acc_ref[i, :, cols] * keep + nt(lhs, p)[:EXTENDED]

    def both(j, scores, maxima, next_scores, next_maxima):
        for cols in halves:
            score(j + 1, next_scores, next_maxima, cols)
            absorb(j, scores, maxima, cols)

    def several(at_once, first):
        def turn(h, carry):
            j = first + at_once * h
            for n in range(0, at_once, 2):
                both(j + n, scores_a, max_a, scores_b, max_b)
                both(j + n + 1, scores_b, max_b, scores_a, max_a)
            return carry

        return turn

    for cols in halves:
        score(0, scores_a, max_a, cols)
    fours = items >> 2
    lax.fori_loop(0, fours, several(4, 0), 0)
    lax.fori_loop(0, (items - 4 * fours + 1) >> 1, several(2, 4 * fours), 0)

    if final:
        sub = lax.broadcasted_iota(jnp.int32, (16, ROWS), 0)
        tail = jnp.zeros((16, ROWS), F32)
        for i in range(BLOCKS):
            sums = acc_ref[i, HEAD_DIM : HEAD_DIM + 1]
            some = sums > 0.0
            safe = jnp.where(some, sums, 1.0)
            logs = jnp.where(some, m_ref[i] + jnp.log2(safe), NEG)
            high = logs.astype(BF16).astype(F32)
            middle = (logs - high).astype(BF16).astype(F32)
            low = logs - high - middle
            out_ref[i * HEAD_DIM : (i + 1) * HEAD_DIM] = (
                acc_ref[i, :HEAD_DIM] * (1.0 / safe)
            ).astype(BF16)
            for n, part in enumerate((high, middle, low)):
                tail = jnp.where(sub == BLOCKS * n + i, part, tail)
        out_ref[PARTIAL:] = tail.astype(BF16)


def attend(meta, order, q, shards, state, partner, final=False):
    steps = tuple(distance for _, distance in shards)
    total = BLOCKS * len(steps)
    starts = state is None
    args = [meta, order] + list(q) + [a for a, _ in shards] + ([] if starts else list(state))
    m_shape, acc_shape = (BLOCKS, 1, ROWS), (BLOCKS, EXTENDED, ROWS)
    if final:
        out_shape = (jax.ShapeDtypeStruct((PARTIAL + 16, ROWS), BF16),)
        work = [pltpu.VMEM(m_shape, F32), pltpu.VMEM(acc_shape, F32)]
    else:
        out_shape = (jax.ShapeDtypeStruct(m_shape, F32), jax.ShapeDtypeStruct(acc_shape, F32))
        work = []
    pairs = BLOCKS * total // 2
    items = BLOCKS * ((total + GROUP - 1) // GROUP) + 8
    got = pl.pallas_call(
        functools.partial(attend_kernel, steps, partner, starts, final),
        out_shape=out_shape,
        in_specs=[SMEM, SMEM] + [VMEM] * (len(args) - 2),
        out_specs=tuple(VMEM for _ in out_shape),
        scratch_shapes=work
        + [
            pltpu.VMEM((total + 1, 2 * BLOCK, HEAD_DIM), BF16),
            pltpu.VMEM((GROUP * BLOCK, ROWS), F32),
            pltpu.VMEM((GROUP * BLOCK, ROWS), F32),
            pltpu.VMEM((1, ROWS), F32),
            pltpu.VMEM((1, ROWS), F32),
            pltpu.SMEM((items,), jnp.int32),
            pltpu.SMEM((64,), jnp.int32),
            pltpu.SMEM((64,), jnp.int32),
            pltpu.SMEM((total + 1,), jnp.int32),
        ]
        + ([pltpu.VMEM((BLOCKS, HEAD_DIM, ROWS), BF16)] if partner else []),
        compiler_params=pltpu.CompilerParams(vmem_limit_bytes=VMEM_BYTES),
        cost_estimate=pl.CostEstimate(
            flops=pairs * 4 * BLOCK * ROWS * 8, bytes_accessed=1 << 18, transcendentals=pairs * 4096
        ),
        name="attend",
    )(*args)
    return got[0] if final else got


def combine_kernel(m_ref, acc_ref, other_ref, out_ref):
    tail = other_ref[PARTIAL:].astype(F32)
    logs = tail[:BLOCKS] + tail[BLOCKS : 2 * BLOCKS] + tail[2 * BLOCKS : 3 * BLOCKS]
    for i in range(BLOCKS):
        sums = acc_ref[i, HEAD_DIM : HEAD_DIM + 1]
        mine = m_ref[i] + jnp.log2(sums)
        theirs = logs[i : i + 1]
        top = jnp.maximum(mine, theirs)
        weight_mine, weight_theirs = jnp.exp2(mine - top), jnp.exp2(theirs - top)
        whole = weight_mine + weight_theirs
        result = acc_ref[i, :HEAD_DIM] * (weight_mine / (sums * whole)) + other_ref[
            i * HEAD_DIM : (i + 1) * HEAD_DIM
        ].astype(F32) * (weight_theirs / whole)
        result = result.astype(BF16)
        for h in range(2):
            out_ref[i, :, h * HEAD_DIM : (h + 1) * HEAD_DIM] = result[
                :, h * BLOCK : (h + 1) * BLOCK
            ].T


def combine(state, other):
    return pl.pallas_call(
        combine_kernel,
        out_shape=jax.ShapeDtypeStruct((BLOCKS, BLOCK, 2 * HEAD_DIM), BF16),
        in_specs=[VMEM] * 3,
        out_specs=VMEM,
        compiler_params=SMALL,
        name="combine",
    )(*state, other)


def pack_kernel(queries_in, keys_in, values_in, out_ref, queries_ref, keys_ref, values_ref, sems):
    pairs = ((queries_in, queries_ref), (keys_in, keys_ref), (values_in, values_ref))
    copies = [pltpu.make_async_copy(a, b, sems.at[n]) for n, (a, b) in enumerate(pairs)]
    for copy in copies:
        copy.start()
    for copy in copies:
        copy.wait()
    for g in range(8):
        keys = keys_ref[:, g * HEAD_DIM : (g + 1) * HEAD_DIM]
        values = values_ref[:, g * HEAD_DIM : (g + 1) * HEAD_DIM]
        for c in range(2):
            first = (2 * g + c) * 2 * HEAD_DIM
            out_ref[8 * c + g, :, : 2 * HEAD_DIM] = queries_ref[:, first : first + 2 * HEAD_DIM]
            out_ref[8 * c + g, :, 2 * HEAD_DIM : 3 * HEAD_DIM] = keys
            out_ref[8 * c + g, :, 3 * HEAD_DIM :] = values


def pack(queries, keys, values):
    rows = queries.shape[0]
    return pl.pallas_call(
        pack_kernel,
        out_shape=jax.ShapeDtypeStruct((16, rows, 4 * HEAD_DIM), BF16),
        in_specs=[pl.BlockSpec(memory_space=pl.ANY)] * 3,
        out_specs=VMEM,
        scratch_shapes=[pltpu.VMEM(a.shape, BF16) for a in (queries, keys, values)]
        + [pltpu.SemaphoreType.DMA((3,))],
        compiler_params=pltpu.CompilerParams(vmem_limit_bytes=56 * 2**20),
        name="pack",
    )(queries, keys, values)


def unpack_kernel(back_ref, out_ref):
    for g in range(8):
        for c in range(2):
            first = (2 * g + c) * 2 * HEAD_DIM
            out_ref[:, first : first + 2 * HEAD_DIM] = back_ref[8 * c + g]


def unpack(back):
    rows = back.shape[1]
    return pl.pallas_call(
        unpack_kernel,
        out_shape=jax.ShapeDtypeStruct((rows, 32 * HEAD_DIM), BF16),
        in_specs=[VMEM],
        out_specs=VMEM,
        compiler_params=SMALL,
        name="unpack",
    )(back)


def body(queries, keys, values, block_order):
    rows = queries.shape[0]
    group = ("c", "yl", "x")
    z_size = lax.axis_size("z")
    meta = jnp.stack([lax.axis_index("yh"), lax.axis_index("z"), lax.axis_index("c")]).astype(jnp.int32)
    got = lax.all_to_all(pack(queries, keys, values), group, 0, 0, tiled=True)
    q, kv = prepare(got.reshape(BLOCKS, BLOCK, 512))

    ring = [(2 * i + k, 2 * ((i + 1 - 2 * k) % z_size) + k) for i in range(z_size) for k in (0, 1)]
    swap = [(0, 1), (1, 0)]

    def onward(a):
        return lax.ppermute(a, ("z", "c"), ring)

    def swapped(a):
        return lax.ppermute(a, "c", swap)

    r1 = onward(kv)
    other_a = lax.ppermute(q[:2], "yh", swap)
    mine = own_start(meta, block_order, q, kv)
    r1, mine, other_a, q = lax.optimization_barrier((r1, mine, other_a, q))

    r2, s1 = onward(r1), swapped(r1)
    other_q = (other_a, lax.ppermute(q[2:], "yh", swap))
    near = [(r1, 1), (s1, -1)]
    r2, other_q = lax.optimization_barrier((r2, other_q))

    r3, s2 = onward(r2), swapped(r2)
    theirs = attend(meta, block_order, other_q, [(kv, 0)] + near, None, True)
    r3, theirs = lax.optimization_barrier((r3, theirs))

    r4, s3 = onward(r3), swapped(r3)
    later = [(r2, 2), (s2, -2), (r3, 3), (s3, -3)]
    theirs = attend(meta, block_order, other_q, later, theirs, True)
    r4, theirs = lax.optimization_barrier((r4, theirs))

    last = [(r4, 4)]
    sent = attend(meta, block_order, other_q, last, theirs, True, True)
    other = lax.ppermute(sent, "yh", swap)
    mine = attend(meta, block_order, (q,), near + later + last, mine, False)
    result = combine(mine, other).reshape(16, rows, 256)
    return unpack(lax.all_to_all(result, group, 0, 0, tiled=True))


def solution(mesh):
    fine = Mesh(mesh.devices.reshape(2, 8, 2, 2, 4), AXES)
    spec = P(AXES, None)
    return jax.shard_map(
        body, mesh=fine, in_specs=(spec, spec, spec, P()), out_specs=spec, check_vma=False
    )
```

```python
import functools

import jax
import jax.numpy as jnp
import numpy as np
from jax import lax
from jax.experimental import pallas as pl
from jax.experimental.pallas import tpu as pltpu
from jax.sharding import Mesh
from jax.sharding import PartitionSpec as P

HEAD_DIM = 128
BLOCK = 256
ROWS = 2 * BLOCK
BLOCKS = 4
EXTENDED = HEAD_DIM + 8
GROUP = 2
PARTIAL = BLOCKS * HEAD_DIM
NEG = -1e30
LOG2E_SCALE = float(np.log2(np.e) / np.sqrt(HEAD_DIM))
AXES = ("yh", "z", "c", "yl", "x")
F32 = jnp.float32
BF16 = jnp.bfloat16
SMEM = pl.BlockSpec(memory_space=pltpu.SMEM)
VMEM = pl.BlockSpec(memory_space=pltpu.VMEM)
VMEM_BYTES = 16 * 2**20
SMALL = pltpu.CompilerParams(vmem_limit_bytes=8 * 2**20)


def nt(a, b):
    return lax.dot_general(a, b, (((1,), (0,)), ((), ())), preferred_element_type=F32)


def prepare_kernel(got_ref, q_ref, kv_ref):
    for b in range(BLOCKS):
        for h in range(2):
            q_ref[b, :, h * BLOCK : (h + 1) * BLOCK] = got_ref[
                b, :, h * HEAD_DIM : (h + 1) * HEAD_DIM
            ].T
        kv_ref[b, :BLOCK] = got_ref[b, :, 2 * HEAD_DIM : 3 * HEAD_DIM]
        value = got_ref[b, :, 3 * HEAD_DIM :].T
        kv_ref[b, BLOCK : BLOCK + HEAD_DIM] = value[:, :HEAD_DIM]
        kv_ref[b, BLOCK + HEAD_DIM :] = value[:, HEAD_DIM:]


def prepare(got):
    return pl.pallas_call(
        prepare_kernel,
        out_shape=(
            jax.ShapeDtypeStruct((BLOCKS, HEAD_DIM, ROWS), BF16),
            jax.ShapeDtypeStruct((BLOCKS, 2 * BLOCK, HEAD_DIM), BF16),
        ),
        in_specs=[VMEM],
        out_specs=(VMEM, VMEM),
        compiler_params=SMALL,
        name="prepare",
    )(got)


def value_of(kv_ref, t):
    return jnp.concatenate(
        [kv_ref[t, BLOCK : BLOCK + HEAD_DIM], kv_ref[t, BLOCK + HEAD_DIM :]], axis=1
    )


def own_kernel(meta_ref, order_ref, q_ref, kv_ref, m_ref, acc_ref):
    first = (meta_ref[0] * 8 + meta_ref[1]) * BLOCKS
    values = jnp.concatenate([value_of(kv_ref, t) for t in range(BLOCKS)], axis=1)
    lhs = jnp.concatenate([values, jnp.ones((16, BLOCKS * BLOCK), BF16)], axis=0)
    keys = jnp.concatenate([kv_ref[t, :BLOCK] for t in range(BLOCKS)], axis=0)
    row = lax.broadcasted_iota(jnp.int32, (BLOCK, ROWS), 0)
    col = lax.broadcasted_iota(jnp.int32, (BLOCK, ROWS), 1) & (BLOCK - 1)
    ahead = row - col
    for i in range(BLOCKS):
        scores = nt(keys, q_ref[i]) * LOG2E_SCALE
        q_pos = order_ref[first + i] * BLOCK
        parts = []
        for t in range(BLOCKS):
            part = scores[t * BLOCK : (t + 1) * BLOCK]
            room = q_pos - order_ref[first + t] * BLOCK
            parts.append(jnp.where(ahead <= room, part, NEG))
        scores = jnp.concatenate(parts, axis=0)
        row_max = jnp.max(scores, axis=0, keepdims=True)
        m_ref[i] = row_max
        acc_ref[i] = nt(lhs, jnp.exp2(scores - row_max).astype(BF16))[:EXTENDED]


def own_start(meta, order, q, kv):
    return pl.pallas_call(
        own_kernel,
        out_shape=(
            jax.ShapeDtypeStruct((BLOCKS, 1, ROWS), F32),
            jax.ShapeDtypeStruct((BLOCKS, EXTENDED, ROWS), F32),
        ),
        in_specs=[SMEM, SMEM, VMEM, VMEM],
        out_specs=(VMEM, VMEM),
        compiler_params=pltpu.CompilerParams(vmem_limit_bytes=VMEM_BYTES),
        cost_estimate=pl.CostEstimate(
            flops=16 * 4 * BLOCK * ROWS * 8, bytes_accessed=1 << 18, transcendentals=1 << 16
        ),
        name="own_start",
    )(meta, order, q, kv)


def attend_kernel(steps, partner, starts, final, *refs):
    shards = len(steps)
    meta_ref, order_ref = refs[:2]
    q_refs, refs = (refs[2:4], refs[4:]) if partner else (refs[2:3], refs[3:])
    kv_refs = refs[:shards]
    rest = refs[shards:]
    if not starts:
        m_in, acc_in = rest[:2]
        rest = rest[2:]
    if final:
        out_ref, rest = rest[0], rest[1:]
    m_ref, acc_ref, kv_s, scores_a, scores_b, max_a, max_b = rest[:7]
    item, slots, before, sorted_k = rest[7:11]
    if partner:
        q_ref = rest[11]
        split = q_refs[0].shape[0]
        q_ref[:split] = q_refs[0][...]
        q_ref[split:] = q_refs[1][...]
    else:
        q_ref = q_refs[0]

    total = BLOCKS * shards
    for n in range(shards):
        kv_s[n * BLOCKS : (n + 1) * BLOCKS] = kv_refs[n][...]
    kv_s[total] = jnp.zeros((2 * BLOCK, HEAD_DIM), BF16)
    if starts:
        m_ref[...] = jnp.full(m_ref.shape, NEG, F32)
        acc_ref[...] = jnp.zeros(acc_ref.shape, F32)
    else:
        m_ref[...] = m_in[...]
        acc_ref[...] = acc_in[...]

    yh, z, c = meta_ref[0], meta_ref[1], meta_ref[2]
    up = 2 * c - 1
    q_side = 1 - yh if partner else yh
    q_pos = [order_ref[(q_side * 8 + z) * BLOCKS + i] for i in range(BLOCKS)]
    k_pos = []
    for distance in steps:
        plane = (z + up * distance + 16) & 7
        k_pos += [order_ref[(yh * 8 + plane) * BLOCKS + b] for b in range(BLOCKS)]

    for p in range(64):
        slots[p] = -1
    for t in range(total):
        slots[k_pos[t]] = t
    count = 0
    for p in range(64):
        found = slots[p]
        sorted_k[count] = found
        before[p] = count
        count = count + jnp.where(found >= 0, 1, 0)

    items = 0
    code = 0
    for i in range(BLOCKS):
        n_seen = before[q_pos[i]]
        mine = (i << 16) | (n_seen << 8)
        for n in range((total + GROUP - 1) // GROUP):
            item[items + n] = mine | (GROUP * n)
        code = jnp.where(n_seen > 0, mine | n_seen, code)
        items = items + ((n_seen + GROUP - 1) >> 1)
    for n in range(3):
        item[items + n] = code

    def places(j):
        code = item[j]
        seen_count, base = (code >> 8) & 255, code & 255
        at = [base + g for g in range(GROUP)]
        blocks = [sorted_k[jnp.maximum(jnp.minimum(n, seen_count - 1), 0)] for n in at]
        return code >> 16, blocks, [n < seen_count for n in at]

    halves = [slice(0, BLOCK), slice(BLOCK, ROWS)]

    def score(j, scores, maxima, cols):
        i, blocks, _ = places(j)
        keys = jnp.concatenate([kv_s[t, :BLOCK] for t in blocks], axis=0)
        s = nt(keys, q_ref[i, :, cols]) * LOG2E_SCALE
        scores[:, cols] = s
        maxima[:, cols] = jnp.max(s, axis=0, keepdims=True)

    def absorb(j, scores, maxima, cols):
        i, blocks, counts = places(j)
        values = [value_of(kv_s, jnp.where(ok, t, total)) for t, ok in zip(blocks, counts)]
        ones = [jnp.full((16, BLOCK), jnp.where(ok, 1.0, 0.0), F32).astype(BF16) for ok in counts]
        lhs = jnp.concatenate([jnp.concatenate(values, axis=1), jnp.concatenate(ones, axis=1)], axis=0)
        old = m_ref[i, :, cols]
        new = jnp.maximum(old, maxima[:, cols])
        keep = jnp.exp2(old - new)
        m_ref[i, :, cols] = new
        p = jnp.exp2(scores[:, cols] - new).astype(BF16)
        acc_ref[i, :, cols] = acc_ref[i, :, cols] * keep + nt(lhs, p)[:EXTENDED]

    def both(j, scores, maxima, next_scores, next_maxima):
        for cols in halves:
            score(j + 1, next_scores, next_maxima, cols)
            absorb(j, scores, maxima, cols)

    def several(at_once, first):
        def turn(h, carry):
            j = first + at_once * h
            for n in range(0, at_once, 2):
                both(j + n, scores_a, max_a, scores_b, max_b)
                both(j + n + 1, scores_b, max_b, scores_a, max_a)
            return carry

        return turn

    for cols in halves:
        score(0, scores_a, max_a, cols)
    fours = items >> 2
    lax.fori_loop(0, fours, several(4, 0), 0)
    lax.fori_loop(0, (items - 4 * fours + 1) >> 1, several(2, 4 * fours), 0)

    if final:
        sub = lax.broadcasted_iota(jnp.int32, (16, ROWS), 0)
        tail = jnp.zeros((16, ROWS), F32)
        for i in range(BLOCKS):
            sums = acc_ref[i, HEAD_DIM : HEAD_DIM + 1]
            some = sums > 0.0
            safe = jnp.where(some, sums, 1.0)
            logs = jnp.where(some, m_ref[i] + jnp.log2(safe), NEG)
            high = logs.astype(BF16).astype(F32)
            middle = (logs - high).astype(BF16).astype(F32)
            low = logs - high - middle
            out_ref[i * HEAD_DIM : (i + 1) * HEAD_DIM] = (
                acc_ref[i, :HEAD_DIM] * (1.0 / safe)
            ).astype(BF16)
            for n, part in enumerate((high, middle, low)):
                tail = jnp.where(sub == BLOCKS * n + i, part, tail)
        out_ref[PARTIAL:] = tail.astype(BF16)


def attend(meta, order, q, shards, state, partner, final=False):
    steps = tuple(distance for _, distance in shards)
    total = BLOCKS * len(steps)
    starts = state is None
    args = [meta, order] + list(q) + [a for a, _ in shards] + ([] if starts else list(state))
    m_shape, acc_shape = (BLOCKS, 1, ROWS), (BLOCKS, EXTENDED, ROWS)
    if final:
        out_shape = (jax.ShapeDtypeStruct((PARTIAL + 16, ROWS), BF16),)
        work = [pltpu.VMEM(m_shape, F32), pltpu.VMEM(acc_shape, F32)]
    else:
        out_shape = (jax.ShapeDtypeStruct(m_shape, F32), jax.ShapeDtypeStruct(acc_shape, F32))
        work = []
    pairs = BLOCKS * total // 2
    items = BLOCKS * ((total + GROUP - 1) // GROUP) + 8
    got = pl.pallas_call(
        functools.partial(attend_kernel, steps, partner, starts, final),
        out_shape=out_shape,
        in_specs=[SMEM, SMEM] + [VMEM] * (len(args) - 2),
        out_specs=tuple(VMEM for _ in out_shape),
        scratch_shapes=work
        + [
            pltpu.VMEM((total + 1, 2 * BLOCK, HEAD_DIM), BF16),
            pltpu.VMEM((GROUP * BLOCK, ROWS), F32),
            pltpu.VMEM((GROUP * BLOCK, ROWS), F32),
            pltpu.VMEM((1, ROWS), F32),
            pltpu.VMEM((1, ROWS), F32),
            pltpu.SMEM((items,), jnp.int32),
            pltpu.SMEM((64,), jnp.int32),
            pltpu.SMEM((64,), jnp.int32),
            pltpu.SMEM((total + 1,), jnp.int32),
        ]
        + ([pltpu.VMEM((BLOCKS, HEAD_DIM, ROWS), BF16)] if partner else []),
        compiler_params=pltpu.CompilerParams(vmem_limit_bytes=VMEM_BYTES),
        cost_estimate=pl.CostEstimate(
            flops=pairs * 4 * BLOCK * ROWS * 8, bytes_accessed=1 << 18, transcendentals=pairs * 4096
        ),
        name="attend",
    )(*args)
    return got[0] if final else got


def combine_kernel(m_ref, acc_ref, other_ref, out_ref):
    tail = other_ref[PARTIAL:].astype(F32)
    logs = tail[:BLOCKS] + tail[BLOCKS : 2 * BLOCKS] + tail[2 * BLOCKS : 3 * BLOCKS]
    for i in range(BLOCKS):
        sums = acc_ref[i, HEAD_DIM : HEAD_DIM + 1]
        mine = m_ref[i] + jnp.log2(sums)
        theirs = logs[i : i + 1]
        top = jnp.maximum(mine, theirs)
        weight_mine, weight_theirs = jnp.exp2(mine - top), jnp.exp2(theirs - top)
        whole = weight_mine + weight_theirs
        result = acc_ref[i, :HEAD_DIM] * (weight_mine / (sums * whole)) + other_ref[
            i * HEAD_DIM : (i + 1) * HEAD_DIM
        ].astype(F32) * (weight_theirs / whole)
        result = result.astype(BF16)
        for h in range(2):
            out_ref[i, :, h * HEAD_DIM : (h + 1) * HEAD_DIM] = result[
                :, h * BLOCK : (h + 1) * BLOCK
            ].T


def combine(state, other):
    return pl.pallas_call(
        combine_kernel,
        out_shape=jax.ShapeDtypeStruct((BLOCKS, BLOCK, 2 * HEAD_DIM), BF16),
        in_specs=[VMEM] * 3,
        out_specs=VMEM,
        compiler_params=SMALL,
        name="combine",
    )(*state, other)


def pack_kernel(queries_in, keys_in, values_in, out_ref, queries_ref, keys_ref, values_ref, sems):
    pairs = ((queries_in, queries_ref), (keys_in, keys_ref), (values_in, values_ref))
    copies = [pltpu.make_async_copy(a, b, sems.at[n]) for n, (a, b) in enumerate(pairs)]
    for copy in copies:
        copy.start()
    for copy in copies:
        copy.wait()
    for g in range(8):
        keys = keys_ref[:, g * HEAD_DIM : (g + 1) * HEAD_DIM]
        values = values_ref[:, g * HEAD_DIM : (g + 1) * HEAD_DIM]
        for c in range(2):
            first = (2 * g + c) * 2 * HEAD_DIM
            out_ref[8 * c + g, :, : 2 * HEAD_DIM] = queries_ref[:, first : first + 2 * HEAD_DIM]
            out_ref[8 * c + g, :, 2 * HEAD_DIM : 3 * HEAD_DIM] = keys
            out_ref[8 * c + g, :, 3 * HEAD_DIM :] = values


def pack(queries, keys, values):
    rows = queries.shape[0]
    return pl.pallas_call(
        pack_kernel,
        out_shape=jax.ShapeDtypeStruct((16, rows, 4 * HEAD_DIM), BF16),
        in_specs=[pl.BlockSpec(memory_space=pl.ANY)] * 3,
        out_specs=VMEM,
        scratch_shapes=[pltpu.VMEM(a.shape, BF16) for a in (queries, keys, values)]
        + [pltpu.SemaphoreType.DMA((3,))],
        compiler_params=pltpu.CompilerParams(vmem_limit_bytes=56 * 2**20),
        name="pack",
    )(queries, keys, values)


def unpack_kernel(back_ref, out_ref):
    for g in range(8):
        for c in range(2):
            first = (2 * g + c) * 2 * HEAD_DIM
            out_ref[:, first : first + 2 * HEAD_DIM] = back_ref[8 * c + g]


def unpack(back):
    rows = back.shape[1]
    return pl.pallas_call(
        unpack_kernel,
        out_shape=jax.ShapeDtypeStruct((rows, 32 * HEAD_DIM), BF16),
        in_specs=[VMEM],
        out_specs=VMEM,
        compiler_params=SMALL,
        name="unpack",
    )(back)


def body(queries, keys, values, block_order):
    rows = queries.shape[0]
    group = ("c", "yl", "x")
    z_size = lax.axis_size("z")
    meta = jnp.stack([lax.axis_index("yh"), lax.axis_index("z"), lax.axis_index("c")]).astype(jnp.int32)
    got = lax.all_to_all(pack(queries, keys, values), group, 0, 0, tiled=True)
    q, kv = prepare(got.reshape(BLOCKS, BLOCK, 512))

    ring = [(2 * i + k, 2 * ((i + 1 - 2 * k) % z_size) + k) for i in range(z_size) for k in (0, 1)]
    swap = [(0, 1), (1, 0)]

    def onward(a):
        return lax.ppermute(a, ("z", "c"), ring)

    def swapped(a):
        return lax.ppermute(a, "c", swap)

    r1 = onward(kv)
    other_a = lax.ppermute(q[:2], "yh", swap)
    mine = own_start(meta, block_order, q, kv)
    r1, mine, other_a, q = lax.optimization_barrier((r1, mine, other_a, q))

    r2, s1 = onward(r1), swapped(r1)
    other_q = (other_a, lax.ppermute(q[2:], "yh", swap))
    near = [(r1, 1), (s1, -1)]
    mine = attend(meta, block_order, (q,), near, mine, False)
    r2, other_q, mine = lax.optimization_barrier((r2, other_q, mine))

    r3, s2 = onward(r2), swapped(r2)
    theirs = attend(meta, block_order, other_q, [(kv, 0)] + near, None, True)
    r3, theirs = lax.optimization_barrier((r3, theirs))

    r4, s3 = onward(r3), swapped(r3)
    later = [(r2, 2), (s2, -2), (r3, 3), (s3, -3)]
    theirs = attend(meta, block_order, other_q, later, theirs, True)
    r4, theirs = lax.optimization_barrier((r4, theirs))

    last = [(r4, 4)]
    sent = attend(meta, block_order, other_q, last, theirs, True, True)
    other = lax.ppermute(sent, "yh", swap)
    mine = attend(meta, block_order, (q,), later + last, mine, False)
    result = combine(mine, other).reshape(16, rows, 256)
    return unpack(lax.all_to_all(result, group, 0, 0, tiled=True))


def solution(mesh):
    fine = Mesh(mesh.devices.reshape(2, 8, 2, 2, 4), AXES)
    spec = P(AXES, None)
    return jax.shard_map(
        body, mesh=fine, in_specs=(spec, spec, spec, P()), out_specs=spec, check_vma=False
    )
```
